32 devices in a mesh: groups: 2 (over x), tm: 16 (over z, y, core).
Axes of the slice: x: 2, y: 2, z: 4, core: 2. Of those that a mesh axis runs over, the one named last changes fastest.
Arguments:
- gauge_series: bfloat16 [2048, 8192], P('groups', 'tm'), parts along dimension 0, may hold values from -6 to 6
- gauge_order: int32 [8192], replicated, may hold values from 0 to 8191, each once
- gauge_block: int32 [8192], replicated, may hold values from 0 to 3
- gauge_weight: bfloat16 [8192, 64], replicated, may hold values from -0.125 to 0.125
- filt_trans: float32 [512, 256], P('groups'), parts along dimension 0, may hold values from -2 to 2
- obs_gain: float32 [512, 256], P('groups'), parts along dimension 0, may hold values from -2 to 2
- smooth_gain: float32 [512, 256], P('groups'), parts along dimension 0, may hold values from -2 to 2
Outputs:
- filtered_mean: float32 [2048, 256], P(('groups', 'tm')), parts along dimension 0
- smoothed_mean: float32 [2048, 256], P(('groups', 'tm')), parts along dimension 0
The draws below stay inside these ranges and needn't reach their ends.
There are 2 independent parts, one for each index of `groups`. The reference program is written for one: setup_inputs(seed, part) draws one part's arguments, and reference() takes and returns one part's arrays. A program takes and returns all parts, laid end to end along the dimension named above; an argument that names none is the same for every part. Nothing has to cross between parts.
Inputs may be any that keep to these rules, and one draw needn't show every extreme that they name: `gauge_order`: each gauge appears in exactly one column.
All inputs are finite; a program needn't handle non-finite values.
Results may differ from the reference program's by a relative error of at most 0.0003.
Values may be sent and summed in bfloat16 or wider, within the bound.
A program may use at most 128 MiB of HBM per device.

```python
import math
import jax
import jax.numpy as jnp
from jax import lax

STATES = 256
BLOCK = 64
GAUGES = 8192
NBLK = 4
TIME = 1024


def spectral_pair(key, salt):
    normal_block = jax.random.normal(jax.random.fold_in(key, salt), (STATES, STATES), jnp.float32)
    eigen_basis, unused_factor = jnp.linalg.qr(normal_block)
    low_rate = math.log(0.2 / TIME)
    high_rate = math.log(1.0 / 30.0)
    log_rates = jax.random.uniform(jax.random.fold_in(key, salt + 1), (STATES,), jnp.float32, low_rate, high_rate)
    skew_block = jax.random.normal(jax.random.fold_in(key, salt + 2), (STATES, STATES), jnp.float32) * (0.4 / math.sqrt(STATES))
    mixing = jnp.eye(STATES, dtype=jnp.float32) + jnp.triu(skew_block, 1)
    return (eigen_basis, mixing, jnp.exp(log_rates))


def conjugated(eigen_basis, mixing, factor):
    scaled = mixing * factor[None, :]
    similar = lax.linalg.triangular_solve(mixing, scaled, left_side=False, lower=False)
    return jnp.dot(jnp.dot(eigen_basis, similar), eigen_basis.T).astype(jnp.float32)


def draw_filt_trans(key, part):
    eigen_basis, mixing, decay_rates = spectral_pair(key, 11)
    return conjugated(eigen_basis, mixing, jnp.exp(-decay_rates))


def draw_obs_gain(key, part):
    eigen_basis, mixing, decay_rates = spectral_pair(key, 11)
    return conjugated(eigen_basis, mixing, jnp.sqrt(-jnp.expm1(-2.0 * decay_rates)))


def draw_smooth_gain(key, part):
    eigen_basis, mixing, decay_rates = spectral_pair(key, 21)
    return conjugated(eigen_basis, mixing, jnp.exp(-decay_rates))


def place_ends(entries, stream_key, smallest, high):
    spot = [jax.random.randint(jax.random.fold_in(stream_key, axis), (), 0, length) for axis, length in enumerate(entries.shape)]
    main_axis = entries.shape.index(max(entries.shape))
    beside = spot[:main_axis] + [(spot[main_axis] + 1) % entries.shape[main_axis]] + spot[main_axis + 1:]
    return entries.at[tuple(spot)].set(smallest).at[tuple(beside)].set(high)


def shard_levels(rng, shape, pieces, low, largest):
    level, own = 1.0, jax.random.fold_in(rng, 6)
    for position, shards_of in pieces:
        heights = jnp.exp(jax.random.uniform(jax.random.fold_in(own, position), (shards_of,), jnp.float32, low / len(pieces), largest / len(pieces)))
        level = level * jnp.repeat(heights, shape[position] // shards_of).reshape([-1 if axis == position else 1 for axis in range(len(shape))])
    return level


def centred(own_key, shape, scale, limit, cuts=(), held_as=jnp.bfloat16):
    entries = jax.random.normal(own_key, shape, jnp.float32) * scale
    if len(cuts) > 0:
        entries = shard_levels(own_key, shape, cuts, -0.22, 0.18) * entries
    return jnp.clip(entries, min=-limit, max=limit).astype(held_as)


def setup_inputs(seed: int = 0, part: int = 0) -> dict:
    seeds = jax.random.split(jax.random.key(seed), 8)
    part_keys = jax.random.split(jax.random.fold_in(seeds[7], part), 8)
    return {
        "gauge_series": centred(part_keys[0], (TIME, GAUGES), 1.0, 6.0, ((1, 16),)),
        "gauge_order": jax.random.permutation(seeds[1], GAUGES).astype(jnp.int32),
        "gauge_block": place_ends(jax.random.randint(seeds[2], (GAUGES,), 0, NBLK), jax.random.fold_in(seeds[2], 1), 0, NBLK - 1).astype(jnp.int32),
        "gauge_weight": centred(seeds[3], (GAUGES, BLOCK), (GAUGES // NBLK) ** -0.5, 0.125),
        "filt_trans": draw_filt_trans(jax.random.fold_in(jax.random.fold_in(seeds[7], part), 71), part),
        "obs_gain": draw_obs_gain(jax.random.fold_in(jax.random.fold_in(seeds[7], part), 71), part),
        "smooth_gain": draw_smooth_gain(jax.random.fold_in(jax.random.fold_in(seeds[7], part), 71), part),
    }


PRECISE = lax.Precision.HIGHEST

def apply_rows(values, matrix):
    return lax.dot_general(values.astype(jnp.float32), matrix.astype(jnp.float32), (((1,), (1,)), ((), ())), precision=PRECISE, preferred_element_type=jnp.float32)

def reference(gauge_series, gauge_order, gauge_block, gauge_weight, filt_trans, obs_gain, smooth_gain):
    blocks = jnp.take(gauge_block, gauge_order)
    weights = jnp.take(gauge_weight, gauge_order, axis=0)
    onehot = (blocks[:, None] == jnp.arange(NBLK, dtype=jnp.int32)[None, :]).astype(jnp.bfloat16)
    design = (onehot[:, :, None] * weights[:, None, :]).reshape(GAUGES, STATES)
    information = jnp.dot(gauge_series.astype(jnp.float32), design.astype(jnp.float32), preferred_element_type=jnp.float32)
    inputs = apply_rows(information, obs_gain)

    def forward(previous, current):
        updated = jnp.dot(filt_trans, previous, precision=PRECISE) + current
        return (updated, updated)
    unused_state, filtered = lax.scan(forward, jnp.zeros((STATES,), jnp.float32), inputs)
    blended = filtered - apply_rows(filtered, smooth_gain)
    blended = blended.at[TIME - 1].set(filtered[TIME - 1])

    def backward(previous, current):
        updated = jnp.dot(smooth_gain, previous, precision=PRECISE) + current
        return (updated, updated)
    unused_back, smoothed = lax.scan(backward, jnp.zeros((STATES,), jnp.float32), blended, reverse=True)
    return (filtered, smoothed)
```

```python
import jax
import jax.numpy as jnp
from jax import lax
from jax.sharding import PartitionSpec as P

PRECISE = lax.Precision.HIGHEST


def matmul(left, right):
    return jnp.dot(left, right, precision=PRECISE, preferred_element_type=jnp.float32)


def shift_down(values, offset):
    zeros = jnp.zeros((offset, values.shape[1]), jnp.float32)
    return jnp.concatenate([zeros, values[:-offset]], 0)


def shift_up(values, offset):
    zeros = jnp.zeros((offset, values.shape[1]), jnp.float32)
    return jnp.concatenate([values[offset:], zeros], 0)


def sweep(values, powers, shift):
    for height, power in enumerate(powers):
        values = values + matmul(shift(values, 1 << height), power)
    return values


def per_device(
    gauge_series, gauge_order, gauge_block, gauge_weight, filt_trans, obs_gain, smooth_gain
):
    states = filt_trans.shape[0]
    devices = lax.axis_size("tm")
    steps = gauge_series.shape[0]
    steps_dev = steps // devices
    columns = gauge_series.shape[1]
    block = gauge_weight.shape[1]
    count_blocks = states // block
    tree_depth = steps_dev.bit_length() - 1
    scan_depth = devices.bit_length() - 1
    position = lax.axis_index("tm")

    mine = lax.dynamic_slice(gauge_order, (position * columns,), (columns,))
    blocks = gauge_block.at[mine].get(mode="promise_in_bounds")
    weights = gauge_weight.at[mine].get(mode="promise_in_bounds")
    chosen = blocks[:, None, None] == jnp.arange(count_blocks, dtype=jnp.int32)[None, :, None]
    design = jnp.where(chosen, weights[:, None, :], jnp.bfloat16(0)).reshape(columns, states)
    information = jnp.dot(gauge_series, design, preferred_element_type=jnp.float32)

    gain = obs_gain.T
    filt = [filt_trans.T]
    back = [smooth_gain.T]
    enter = filt[0] - matmul(filt[0], back[0])
    crossed = []
    for height in range(tree_depth):
        pair = matmul(jnp.concatenate([enter, back[-1]], 0), back[-1])
        crossed.append(pair[:states])
        back.append(pair[states:])
        wide = matmul(filt[-1], jnp.concatenate([filt[-1], crossed[-1]], 1))
        filt.append(wide[:, :states])
        enter = enter + wide[:, states:]
    for height in range(scan_depth - 1):
        filt.append(matmul(filt[-1], filt[-1]))
        back.append(matmul(back[-1], back[-1]))

    ends = matmul(information, gain)
    starts = ends - matmul(ends, back[0])
    for height in range(tree_depth):
        ends = ends.reshape(-1, 2, states)
        starts = starts.reshape(-1, 2, states)
        wide = matmul(ends[:, 0], jnp.concatenate([filt[height], crossed[height]], 1))
        starts = starts[:, 0] + wide[:, states:] + matmul(starts[:, 1], back[height])
        ends = ends[:, 1] + wide[:, :states]

    reached = sweep(ends, filt[tree_depth : tree_depth + scan_depth], shift_down)
    arrive = shift_down(reached, 1)
    final = reached[-1:]
    starts = starts + matmul(arrive, enter)
    last = jnp.zeros((devices - 1, states), jnp.float32)
    starts = starts + jnp.concatenate([last, matmul(final, back[tree_depth])], 0)
    returned = sweep(starts, back[tree_depth : tree_depth + scan_depth], shift_up)
    arrive_back = jnp.concatenate([returned[1:], final], 0)

    packed = jnp.concatenate(
        [
            information.reshape(devices, steps_dev, states),
            arrive[:, None],
            arrive_back[:, None],
            jnp.zeros((devices, 6, states), jnp.float32),
        ],
        1,
    )
    parts = lax.all_to_all(packed, "tm", split_axis=0, concat_axis=0, tiled=True)
    total = jnp.sum(parts, 0)
    entering = total[steps_dev : steps_dev + 1]
    entering_back = total[steps_dev + 1 : steps_dev + 2]

    inputs = matmul(total[:steps_dev], gain)
    inputs = inputs + jnp.concatenate(
        [matmul(entering, filt[0]), jnp.zeros((steps_dev - 1, states), jnp.float32)], 0
    )
    filtered = sweep(inputs, filt[:tree_depth], shift_down)
    following = jnp.concatenate(
        [jnp.zeros((steps_dev - 1, states), jnp.float32), entering_back], 0
    )
    blended = filtered + matmul(following - filtered, back[0])
    smoothed = sweep(blended, back[:tree_depth], shift_up)
    return (filtered, smoothed)


def solution(mesh):
    placed = (
        P("groups", "tm"),
        P(),
        P(),
        P(),
        P("groups", None),
        P("groups", None),
        P("groups", None),
    )
    return jax.shard_map(
        per_device,
        mesh=mesh,
        in_specs=placed,
        out_specs=(P(("groups", "tm"), None), P(("groups", "tm"), None)),
        check_vma=False,
    )
```

```python
import functools

import jax
import jax.numpy as jnp
from jax import lax
from jax.experimental import pallas as pl
from jax.experimental.pallas import tpu as pltpu
from jax.sharding import PartitionSpec as P

PRECISE = lax.Precision.HIGHEST
MESH = pl.DeviceIdType.MESH
LANES = 128


def matmul(left, right):
    return jnp.dot(left, right, precision=PRECISE, preferred_element_type=jnp.float32)


def shift(values, offset):
    rows = values.shape[0]
    moved = pltpu.roll(values, offset % rows, 0)
    place = lax.broadcasted_iota(jnp.int32, values.shape, 0)
    kept = place >= offset if offset > 0 else place < rows + offset
    return jnp.where(kept, moved, 0.0)


def put_row(values, row, where):
    place = lax.broadcasted_iota(jnp.int32, values.shape, 0)
    return values + jnp.where(place == where, row, 0.0)


def bit_reversed(number, bits):
    return int(format(number, "b").zfill(bits)[::-1], 2) if bits else 0


def kernel(
    devices,
    series_ref,
    order_ref,
    block_ref,
    weight_ref,
    filt_in,
    gain_in,
    back_in,
    filtered_ref,
    smoothed_ref,
    info,
    half,
    land,
    carry,
    carry_land,
    filt,
    back,
    crossed,
    enter,
    gain,
    ends,
    starts,
    small,
    sib_send,
    sib_recv,
    info_send,
    info_recv,
    carry_send,
    carry_recv,
):
    me = lax.axis_index("tm")
    core = lax.rem(me, 2)
    chip = lax.div(me, 2)
    sibling = me + 1 - 2 * core
    chips = devices // 2
    steps = series_ref.shape[0]
    length = steps // devices
    states = filt_in.shape[0]
    gauges = weight_ref.shape[1]
    block = weight_ref.shape[0]
    depth = length.bit_length() - 1
    scans = devices.bit_length() - 1
    halves = states // LANES

    barrier = pltpu.get_barrier_semaphore()
    for k in range(1, devices):
        pl.semaphore_signal(
            barrier, inc=1, device_id={"tm": lax.rem(me + k, devices)}, device_id_type=MESH
        )

    order = order_ref[me]
    piece = min(1024, gauges)
    gathered = None
    for base in range(0, gauges, piece):
        spot = lax.broadcasted_iota(jnp.int32, (piece, order.shape[1]), 0) + base
        onehot = jnp.where(spot == order, 1.0, 0.0).astype(jnp.bfloat16)
        blocks = block_ref[:, base : base + piece].astype(jnp.float32)
        blocks = jnp.broadcast_to(blocks, (16, piece)).astype(jnp.bfloat16)
        table = jnp.concatenate([weight_ref[:, base : base + piece], blocks], 0)
        part = jnp.dot(table, onehot, preferred_element_type=jnp.float32)
        gathered = part if gathered is None else gathered + part
    weights = gathered[:block]
    number = gathered[block : block + 1]
    design = jnp.concatenate(
        [jnp.where(number == float(k), weights, 0.0) for k in range(states // block)], 0
    ).astype(jnp.bfloat16)
    chunk = min(steps, 1024)
    for base in range(0, steps, chunk):
        partial = lax.dot_general(
            series_ref[base : base + chunk],
            design,
            (((1,), (1,)), ((), ())),
            preferred_element_type=jnp.float32,
        )
        for b in range(base // length, (base + chunk) // length):
            at = ((b % 2) * chips + b // 2) * length
            row = b * length - base
            for j in range(halves):
                info[j, at : at + length] = partial[
                    row : row + length, j * LANES : (j + 1) * LANES
                ]

    pl.semaphore_wait(barrier, devices - 1)
    sib = []
    for k in range(chips):
        target = lax.rem(chip + k, chips)
        rows = pl.ds(pl.multiple_of(((1 - core) * chips + target) * length, length), length)
        copy = pltpu.make_async_remote_copy(
            src_ref=info.at[:, rows],
            dst_ref=half.at[k],
            send_sem=sib_send.at[k],
            recv_sem=sib_recv.at[k],
            device_id={"tm": sibling},
            device_id_type=MESH,
        )
        copy.start()
        sib.append(copy)

    for t in range(length):
        at = bit_reversed(t, depth) * devices
        for c in range(2):
            for j in range(halves):
                ends[at + c * chips : at + (c + 1) * chips, j * LANES : (j + 1) * LANES] = info[
                    j, pl.ds(c * chips * length + t, chips, stride=length)
                ]

    gain[...] = gain_in[...].T
    filt[0] = filt_in[...].T
    back[0] = back_in[...].T
    enter[...] = filt[0] - matmul(filt[0], back[0])

    sends = []
    for k in range(chips):
        sib[k].wait()
        target = lax.rem(chip + k, chips)
        rows = pl.ds(pl.multiple_of((core * chips + target) * length, length), length)
        half[k] = half[k] + info[:, rows]
        if k > 0:
            copy = pltpu.make_async_remote_copy(
                src_ref=half.at[k],
                dst_ref=land.at[k],
                send_sem=info_send.at[k],
                recv_sem=info_recv.at[k],
                device_id={"tm": 2 * target + core},
                device_id_type=MESH,
            )
            copy.start()
            sends.append(copy)

    for h in range(depth):
        crossed[h] = matmul(enter[...], back[h])
        back[h + 1] = matmul(back[h], back[h])
        filt[h + 1] = matmul(filt[h], filt[h])
        enter[...] = enter[...] + matmul(filt[h], crossed[h])
    for h in range(depth, depth + scans - 1):
        filt[h + 1] = matmul(filt[h], filt[h])
        back[h + 1] = matmul(back[h], back[h])

    for base in range(0, steps, chunk):
        here = slice(base, base + chunk)
        ends[here] = matmul(ends[here], gain[...])
        starts[here] = ends[here] - matmul(ends[here], back[0])
    rows = steps
    for h in range(depth):
        rows //= 2
        part = min(rows, chunk)
        for base in range(0, rows, part):
            here = slice(base, base + part)
            there = slice(rows + base, rows + base + part)
            left = ends[here]
            starts[here] = (
                starts[here] + matmul(starts[there], back[h]) + matmul(left, crossed[h])
            )
            ends[here] = ends[there] + matmul(left, filt[h])

    for b in range(devices):
        source = (b % 2) * chips + b // 2
        small[0, b : b + 1] = ends[source : source + 1]
        small[1, b : b + 1] = starts[source : source + 1]
    reached = small[0]
    opened = small[1]
    for h in range(scans):
        reached = reached + matmul(shift(reached, 1 << h), filt[depth + h])
    arrive = shift(reached, 1)
    final = reached[devices - 1 : devices]
    opened = opened + matmul(arrive, enter[...])
    leaving = put_row(jnp.zeros_like(opened), final, devices - 1)
    opened = opened + matmul(leaving, back[depth])
    for h in range(scans):
        opened = opened + matmul(shift(opened, -(1 << h)), back[depth + h])
    arrive_back = put_row(shift(opened, -1), final, devices - 1)
    for b in range(devices):
        carry[b, 0:1] = arrive[b : b + 1]
        carry[b, 1:2] = arrive_back[b : b + 1]

    carries = []
    for k in range(1, devices):
        target = lax.rem(me + k, devices)
        copy = pltpu.make_async_remote_copy(
            src_ref=carry.at[target],
            dst_ref=carry_land.at[k],
            send_sem=carry_send.at[k],
            recv_sem=carry_recv.at[k],
            device_id={"tm": target},
            device_id_type=MESH,
        )
        copy.start()
        carries.append(copy)

    total = half[0]
    for k, copy in enumerate(sends):
        copy.wait()
        total = total + land[k + 1]
    total = jnp.concatenate([total[j] for j in range(halves)], 1)
    inputs = matmul(total, gain[...])

    entering = carry[me]
    for k, copy in enumerate(carries):
        copy.wait()
        entering = entering + carry_land[k + 1]

    first = put_row(jnp.zeros_like(inputs), entering[0:1], 0)
    filtered = inputs + matmul(first, filt[0])
    for h in range(depth):
        filtered = filtered + matmul(shift(filtered, 1 << h), filt[h])
    filtered_ref[...] = filtered
    following = put_row(jnp.zeros_like(inputs), entering[1:2], length - 1)
    smoothed = filtered + matmul(following - filtered, back[0])
    for h in range(depth):
        smoothed = smoothed + matmul(shift(smoothed, -(1 << h)), back[h])
    smoothed_ref[...] = smoothed


def per_device(
    gauge_series, gauge_order, gauge_block, gauge_weight, filt_trans, obs_gain, smooth_gain
):
    devices = lax.axis_size("tm")
    steps, columns = gauge_series.shape
    states = filt_trans.shape[0]
    length = steps // devices
    chips = devices // 2
    depth = length.bit_length() - 1
    scans = devices.bit_length() - 1
    halves = states // LANES
    out = jax.ShapeDtypeStruct((length, states), jnp.float32)
    square = (states, states)
    return pl.pallas_call(
        functools.partial(kernel, devices),
        out_shape=(out, out),
        in_specs=[pl.BlockSpec(memory_space=pltpu.VMEM)] * 7,
        out_specs=[pl.BlockSpec(memory_space=pltpu.VMEM)] * 2,
        scratch_shapes=[
            pltpu.VMEM((halves, steps, LANES), jnp.float32),
            pltpu.VMEM((chips, halves, length, LANES), jnp.float32),
            pltpu.VMEM((chips, halves, length, LANES), jnp.float32),
            pltpu.VMEM((devices, 2, states), jnp.float32),
            pltpu.VMEM((devices, 2, states), jnp.float32),
            pltpu.VMEM((depth + scans,) + square, jnp.float32),
            pltpu.VMEM((depth + scans,) + square, jnp.float32),
            pltpu.VMEM((depth,) + square, jnp.float32),
            pltpu.VMEM(square, jnp.float32),
            pltpu.VMEM(square, jnp.float32),
            pltpu.VMEM((steps, states), jnp.float32),
            pltpu.VMEM((steps, states), jnp.float32),
            pltpu.VMEM((2, devices, states), jnp.float32),
            pltpu.SemaphoreType.DMA((chips,)),
            pltpu.SemaphoreType.DMA((chips,)),
            pltpu.SemaphoreType.DMA((chips,)),
            pltpu.SemaphoreType.DMA((chips,)),
            pltpu.SemaphoreType.DMA((devices,)),
            pltpu.SemaphoreType.DMA((devices,)),
        ],
        compiler_params=pltpu.CompilerParams(
            collective_id=0, has_side_effects=True, vmem_limit_bytes=56 << 20
        ),
    )(
        gauge_series,
        gauge_order.reshape(devices, 1, columns),
        gauge_block.reshape(1, -1),
        gauge_weight.T,
        filt_trans,
        obs_gain,
        smooth_gain,
    )


def solution(mesh):
    placed = (
        P("groups", "tm"),
        P(),
        P(),
        P(),
        P("groups", None),
        P("groups", None),
        P("groups", None),
    )
    return jax.shard_map(
        per_device,
        mesh=mesh,
        in_specs=placed,
        out_specs=(P(("groups", "tm"), None), P(("groups", "tm"), None)),
        check_vma=False,
    )
```

```python
import functools

import jax
import jax.numpy as jnp
from jax import lax
from jax.experimental import pallas as pl
from jax.experimental.pallas import tpu as pltpu
from jax.sharding import PartitionSpec as P

PRECISE = lax.Precision.HIGHEST
MESH = pl.DeviceIdType.MESH
LANES = 128


def matmul(left, right):
    return jnp.dot(left, right, precision=PRECISE, preferred_element_type=jnp.float32)


def split(values):
    high = values.astype(jnp.bfloat16)
    return high, (values - high.astype(jnp.float32)).astype(jnp.bfloat16)


def matmul3(left, right):
    high, low = split(left)
    top, rest = split(right)
    cross = jnp.dot(high, rest, preferred_element_type=jnp.float32)
    cross = cross + jnp.dot(low, top, preferred_element_type=jnp.float32)
    return cross + jnp.dot(high, top, preferred_element_type=jnp.float32)


def shift(values, offset):
    rows = values.shape[0]
    moved = pltpu.roll(values, offset % rows, 0)
    place = lax.broadcasted_iota(jnp.int32, values.shape, 0)
    kept = place >= offset if offset > 0 else place < rows + offset
    return jnp.where(kept, moved, 0.0)


def put_row(values, row, where):
    place = lax.broadcasted_iota(jnp.int32, values.shape, 0)
    return values + jnp.where(place == where, row, 0.0)


def bit_reversed(number, bits):
    return int(format(number, "b").zfill(bits)[::-1], 2) if bits else 0


def kernel(
    devices,
    series_ref,
    order_ref,
    block_ref,
    weight_ref,
    filt_in,
    gain_in,
    back_in,
    filtered_ref,
    smoothed_ref,
    info,
    half,
    land,
    carry,
    carry_land,
    filt,
    back,
    crossed,
    enter,
    gain,
    ends,
    starts,
    small,
    sib_send,
    sib_recv,
    info_send,
    info_recv,
    carry_send,
    carry_recv,
):
    me = lax.axis_index("tm")
    core = lax.rem(me, 2)
    chip = lax.div(me, 2)
    sibling = me + 1 - 2 * core
    chips = devices // 2
    steps = series_ref.shape[0]
    length = steps // devices
    states = filt_in.shape[0]
    gauges = weight_ref.shape[1]
    block = weight_ref.shape[0]
    depth = length.bit_length() - 1
    scans = devices.bit_length() - 1
    halves = states // LANES

    barrier = pltpu.get_barrier_semaphore()
    for k in range(1, devices):
        pl.semaphore_signal(
            barrier, inc=1, device_id={"tm": lax.rem(me + k, devices)}, device_id_type=MESH
        )

    order = order_ref[me]
    piece = min(1024, gauges)
    gathered = None
    for base in range(0, gauges, piece):
        spot = lax.broadcasted_iota(jnp.int32, (piece, order.shape[1]), 0) + base
        onehot = jnp.where(spot == order, 1.0, 0.0).astype(jnp.bfloat16)
        blocks = block_ref[:, base : base + piece].astype(jnp.float32)
        blocks = jnp.broadcast_to(blocks, (16, piece)).astype(jnp.bfloat16)
        table = jnp.concatenate([weight_ref[:, base : base + piece], blocks], 0)
        part = jnp.dot(table, onehot, preferred_element_type=jnp.float32)
        gathered = part if gathered is None else gathered + part
    weights = gathered[:block]
    number = gathered[block : block + 1]
    design = jnp.concatenate(
        [jnp.where(number == float(k), weights, 0.0) for k in range(states // block)], 0
    ).astype(jnp.bfloat16)
    chunk = min(steps, 1024)
    for base in range(0, steps, chunk):
        partial = lax.dot_general(
            series_ref[base : base + chunk],
            design,
            (((1,), (1,)), ((), ())),
            preferred_element_type=jnp.float32,
        )
        for b in range(base // length, (base + chunk) // length):
            at = ((b % 2) * chips + b // 2) * length
            row = b * length - base
            for j in range(halves):
                info[j, at : at + length] = partial[
                    row : row + length, j * LANES : (j + 1) * LANES
                ]

    pl.semaphore_wait(barrier, devices - 1)
    sib = []
    for k in range(chips):
        target = lax.rem(chip + k, chips)
        rows = pl.ds(pl.multiple_of(((1 - core) * chips + target) * length, length), length)
        copy = pltpu.make_async_remote_copy(
            src_ref=info.at[:, rows],
            dst_ref=half.at[k],
            send_sem=sib_send.at[k],
            recv_sem=sib_recv.at[k],
            device_id={"tm": sibling},
            device_id_type=MESH,
        )
        copy.start()
        sib.append(copy)

    for t in range(length):
        at = bit_reversed(t, depth) * devices
        for c in range(2):
            for j in range(halves):
                ends[at + c * chips : at + (c + 1) * chips, j * LANES : (j + 1) * LANES] = info[
                    j, pl.ds(c * chips * length + t, chips, stride=length)
                ]

    gain[...] = gain_in[...].T
    filt[0] = filt_in[...].T
    back[0] = back_in[...].T
    enter[...] = filt[0] - matmul(filt[0], back[0])

    sends = []
    for k in range(chips):
        sib[k].wait()
        target = lax.rem(chip + k, chips)
        rows = pl.ds(pl.multiple_of((core * chips + target) * length, length), length)
        half[k] = half[k] + info[:, rows]
        if k > 0:
            copy = pltpu.make_async_remote_copy(
                src_ref=half.at[k],
                dst_ref=land.at[k],
                send_sem=info_send.at[k],
                recv_sem=info_recv.at[k],
                device_id={"tm": 2 * target + core},
                device_id_type=MESH,
            )
            copy.start()
            sends.append(copy)

    for h in range(depth):
        crossed[h] = matmul3(enter[...], back[h])
        back[h + 1] = matmul(back[h], back[h])
        filt[h + 1] = matmul(filt[h], filt[h])
        enter[...] = enter[...] + matmul3(filt[h], crossed[h])
    for h in range(depth, depth + scans - 1):
        filt[h + 1] = matmul(filt[h], filt[h])
        back[h + 1] = matmul(back[h], back[h])

    for base in range(0, steps, chunk):
        here = slice(base, base + chunk)
        ends[here] = matmul3(ends[here], gain[...])
        starts[here] = ends[here] - matmul3(ends[here], back[0])
    rows = steps
    for h in range(depth):
        rows //= 2
        part = min(rows, chunk)
        for base in range(0, rows, part):
            here = slice(base, base + part)
            there = slice(rows + base, rows + base + part)
            left = ends[here]
            starts[here] = (
                starts[here] + matmul3(starts[there], back[h]) + matmul3(left, crossed[h])
            )
            ends[here] = ends[there] + matmul3(left, filt[h])

    for b in range(devices):
        source = (b % 2) * chips + b // 2
        small[0, b : b + 1] = ends[source : source + 1]
        small[1, b : b + 1] = starts[source : source + 1]
    reached = small[0]
    opened = small[1]
    for h in range(scans):
        reached = reached + matmul3(shift(reached, 1 << h), filt[depth + h])
    arrive = shift(reached, 1)
    final = reached[devices - 1 : devices]
    opened = opened + matmul3(arrive, enter[...])
    leaving = put_row(jnp.zeros_like(opened), final, devices - 1)
    opened = opened + matmul3(leaving, back[depth])
    for h in range(scans):
        opened = opened + matmul3(shift(opened, -(1 << h)), back[depth + h])
    arrive_back = put_row(shift(opened, -1), final, devices - 1)
    for b in range(devices):
        carry[b, 0:1] = arrive[b : b + 1]
        carry[b, 1:2] = arrive_back[b : b + 1]

    carries = []
    for k in range(1, devices):
        target = lax.rem(me + k, devices)
        copy = pltpu.make_async_remote_copy(
            src_ref=carry.at[target],
            dst_ref=carry_land.at[k],
            send_sem=carry_send.at[k],
            recv_sem=carry_recv.at[k],
            device_id={"tm": target},
            device_id_type=MESH,
        )
        copy.start()
        carries.append(copy)

    total = half[0]
    for k, copy in enumerate(sends):
        copy.wait()
        total = total + land[k + 1]
    total = jnp.concatenate([total[j] for j in range(halves)], 1)
    inputs = matmul3(total, gain[...])

    entering = carry[me]
    for k, copy in enumerate(carries):
        copy.wait()
        entering = entering + carry_land[k + 1]

    first = put_row(jnp.zeros_like(inputs), entering[0:1], 0)
    filtered = inputs + matmul3(first, filt[0])
    for h in range(depth):
        filtered = filtered + matmul3(shift(filtered, 1 << h), filt[h])
    filtered_ref[...] = filtered
    following = put_row(jnp.zeros_like(inputs), entering[1:2], length - 1)
    smoothed = filtered + matmul3(following - filtered, back[0])
    for h in range(depth):
        smoothed = smoothed + matmul3(shift(smoothed, -(1 << h)), back[h])
    smoothed_ref[...] = smoothed


def per_device(
    gauge_series, gauge_order, gauge_block, gauge_weight, filt_trans, obs_gain, smooth_gain
):
    devices = lax.axis_size("tm")
    steps, columns = gauge_series.shape
    states = filt_trans.shape[0]
    length = steps // devices
    chips = devices // 2
    depth = length.bit_length() - 1
    scans = devices.bit_length() - 1
    halves = states // LANES
    out = jax.ShapeDtypeStruct((length, states), jnp.float32)
    square = (states, states)
    return pl.pallas_call(
        functools.partial(kernel, devices),
        out_shape=(out, out),
        in_specs=[pl.BlockSpec(memory_space=pltpu.VMEM)] * 7,
        out_specs=[pl.BlockSpec(memory_space=pltpu.VMEM)] * 2,
        scratch_shapes=[
            pltpu.VMEM((halves, steps, LANES), jnp.float32),
            pltpu.VMEM((chips, halves, length, LANES), jnp.float32),
            pltpu.VMEM((chips, halves, length, LANES), jnp.float32),
            pltpu.VMEM((devices, 2, states), jnp.float32),
            pltpu.VMEM((devices, 2, states), jnp.float32),
            pltpu.VMEM((depth + scans,) + square, jnp.float32),
            pltpu.VMEM((depth + scans,) + square, jnp.float32),
            pltpu.VMEM((depth,) + square, jnp.float32),
            pltpu.VMEM(square, jnp.float32),
            pltpu.VMEM(square, jnp.float32),
            pltpu.VMEM((steps, states), jnp.float32),
            pltpu.VMEM((steps, states), jnp.float32),
            pltpu.VMEM((2, devices, states), jnp.float32),
            pltpu.SemaphoreType.DMA((chips,)),
            pltpu.SemaphoreType.DMA((chips,)),
            pltpu.SemaphoreType.DMA((chips,)),
            pltpu.SemaphoreType.DMA((chips,)),
            pltpu.SemaphoreType.DMA((devices,)),
            pltpu.SemaphoreType.DMA((devices,)),
        ],
        compiler_params=pltpu.CompilerParams(
            collective_id=0, has_side_effects=True, vmem_limit_bytes=56 << 20
        ),
    )(
        gauge_series,
        gauge_order.reshape(devices, 1, columns),
        gauge_block.reshape(1, -1),
        gauge_weight.T,
        filt_trans,
        obs_gain,
        smooth_gain,
    )


def solution(mesh):
    placed = (
        P("groups", "tm"),
        P(),
        P(),
        P(),
        P("groups", None),
        P("groups", None),
        P("groups", None),
    )
    return jax.shard_map(
        per_device,
        mesh=mesh,
        in_specs=placed,
        out_specs=(P(("groups", "tm"), None), P(("groups", "tm"), None)),
        check_vma=False,
    )
```

```python
import functools

import jax
import jax.numpy as jnp
from jax import lax
from jax.experimental import pallas as pl
from jax.experimental.pallas import tpu as pltpu
from jax.sharding import PartitionSpec as P

PRECISE = lax.Precision.HIGHEST
MESH = pl.DeviceIdType.MESH
LANES = 128


def matmul(left, right):
    return jnp.dot(left, right, precision=PRECISE, preferred_element_type=jnp.float32)


def split(values):
    high = values.astype(jnp.bfloat16)
    return high, (values - high.astype(jnp.float32)).astype(jnp.bfloat16)


def matmul3(left, right):
    high, low = split(left)
    top, rest = split(right)
    cross = jnp.dot(high, rest, preferred_element_type=jnp.float32)
    cross = cross + jnp.dot(low, top, preferred_element_type=jnp.float32)
    return cross + jnp.dot(high, top, preferred_element_type=jnp.float32)


def shift(values, offset):
    rows = values.shape[0]
    moved = pltpu.roll(values, offset % rows, 0)
    place = lax.broadcasted_iota(jnp.int32, values.shape, 0)
    kept = place >= offset if offset > 0 else place < rows + offset
    return jnp.where(kept, moved, 0.0)


def put_row(values, row, where):
    place = lax.broadcasted_iota(jnp.int32, values.shape, 0)
    return values + jnp.where(place == where, row, 0.0)


def bit_reversed(number, bits):
    return int(format(number, "b").zfill(bits)[::-1], 2) if bits else 0


def kernel(
    devices,
    series_ref,
    order_ref,
    block_ref,
    weight_ref,
    filt_in,
    gain_in,
    back_in,
    filtered_ref,
    smoothed_ref,
    info,
    half,
    land,
    carry,
    carry_land,
    filt,
    back,
    crossed,
    enter,
    gain,
    ends,
    starts,
    small,
    sib_send,
    sib_recv,
    info_send,
    info_recv,
    carry_send,
    carry_recv,
):
    me = lax.axis_index("tm")
    core = lax.rem(me, 2)
    chip = lax.div(me, 2)
    sibling = me + 1 - 2 * core
    chips = devices // 2
    steps = series_ref.shape[0]
    length = steps // devices
    states = filt_in.shape[0]
    gauges = weight_ref.shape[1]
    block = weight_ref.shape[0]
    depth = length.bit_length() - 1
    scans = devices.bit_length() - 1
    halves = states // LANES

    barrier = pltpu.get_barrier_semaphore()
    for k in range(1, devices):
        pl.semaphore_signal(
            barrier, inc=1, device_id={"tm": lax.rem(me + k, devices)}, device_id_type=MESH
        )

    order = order_ref[me]
    piece = min(1024, gauges)
    gathered = None
    for base in range(0, gauges, piece):
        spot = lax.broadcasted_iota(jnp.int32, (piece, order.shape[1]), 0)
        onehot = jnp.where(spot == order - base, 1.0, 0.0).astype(jnp.bfloat16)
        blocks = block_ref[:, base : base + piece].astype(jnp.float32)
        blocks = jnp.broadcast_to(blocks, (16, piece)).astype(jnp.bfloat16)
        table = jnp.concatenate([weight_ref[:, base : base + piece], blocks], 0)
        part = jnp.dot(table, onehot, preferred_element_type=jnp.float32)
        gathered = part if gathered is None else gathered + part
    weights = gathered[:block]
    number = gathered[block : block + 1]
    design = jnp.concatenate(
        [jnp.where(number == float(k), weights, 0.0) for k in range(states // block)], 0
    ).astype(jnp.bfloat16)
    chunk = min(steps, 1024)
    for base in range(0, steps, chunk):
        partial = lax.dot_general(
            series_ref[base : base + chunk],
            design,
            (((1,), (1,)), ((), ())),
            preferred_element_type=jnp.float32,
        )
        for b in range(base // length, (base + chunk) // length):
            at = ((b % 2) * chips + b // 2) * length
            row = b * length - base
            for j in range(halves):
                info[j, at : at + length] = partial[
                    row : row + length, j * LANES : (j + 1) * LANES
                ]

    pl.semaphore_wait(barrier, devices - 1)
    sib = []
    for k in range(chips):
        target = lax.rem(chip + k, chips)
        rows = pl.ds(pl.multiple_of(((1 - core) * chips + target) * length, length), length)
        copy = pltpu.make_async_remote_copy(
            src_ref=info.at[:, rows],
            dst_ref=half.at[k],
            send_sem=sib_send.at[k],
            recv_sem=sib_recv.at[k],
            device_id={"tm": sibling},
            device_id_type=MESH,
        )
        copy.start()
        sib.append(copy)

    for t in range(length):
        at = bit_reversed(t, depth) * devices
        for c in range(2):
            for j in range(halves):
                ends[at + c * chips : at + (c + 1) * chips, j * LANES : (j + 1) * LANES] = info[
                    j, pl.ds(c * chips * length + t, chips, stride=length)
                ]

    gain[...] = gain_in[...].T
    filt[0] = filt_in[...].T
    back[0] = back_in[...].T

    sends = []
    for k in range(chips):
        sib[k].wait()
        target = lax.rem(chip + k, chips)
        rows = pl.ds(pl.multiple_of((core * chips + target) * length, length), length)
        half[k] = half[k] + info[:, rows]
        if k > 0:
            copy = pltpu.make_async_remote_copy(
                src_ref=half.at[k],
                dst_ref=land.at[k],
                send_sem=info_send.at[k],
                recv_sem=info_recv.at[k],
                device_id={"tm": 2 * target + core},
                device_id_type=MESH,
            )
            copy.start()
            sends.append(copy)

    enter[...] = filt[0] - matmul(filt[0], back[0])
    for h in range(depth):
        crossed[h] = matmul3(enter[...], back[h])
        back[h + 1] = matmul(back[h], back[h])
        filt[h + 1] = matmul(filt[h], filt[h])
        enter[...] = enter[...] + matmul3(filt[h], crossed[h])
    for h in range(depth, depth + scans - 1):
        filt[h + 1] = matmul(filt[h], filt[h])
        back[h + 1] = matmul(back[h], back[h])

    for base in range(0, steps, chunk):
        here = slice(base, base + chunk)
        ends[here] = matmul3(ends[here], gain[...])
        starts[here] = ends[here] - matmul3(ends[here], back[0])
    rows = steps
    for h in range(depth):
        rows //= 2
        part = min(rows, chunk)
        for base in range(0, rows, part):
            here = slice(base, base + part)
            there = slice(rows + base, rows + base + part)
            left = ends[here]
            starts[here] = (
                starts[here] + matmul3(starts[there], back[h]) + matmul3(left, crossed[h])
            )
            ends[here] = ends[there] + matmul3(left, filt[h])

    for b in range(devices):
        source = (b % 2) * chips + b // 2
        small[0, b : b + 1] = ends[source : source + 1]
        small[1, b : b + 1] = starts[source : source + 1]
    reached = small[0]
    opened = small[1]
    for h in range(scans):
        reached = reached + matmul3(shift(reached, 1 << h), filt[depth + h])
    arrive = shift(reached, 1)
    final = reached[devices - 1 : devices]
    opened = opened + matmul3(arrive, enter[...])
    leaving = put_row(jnp.zeros_like(opened), final, devices - 1)
    opened = opened + matmul3(leaving, back[depth])
    for h in range(scans):
        opened = opened + matmul3(shift(opened, -(1 << h)), back[depth + h])
    arrive_back = put_row(shift(opened, -1), final, devices - 1)
    for b in range(devices):
        carry[b, 0:1] = arrive[b : b + 1]
        carry[b, 1:2] = arrive_back[b : b + 1]

    carries = []
    for k in range(1, devices):
        target = lax.rem(me + k, devices)
        copy = pltpu.make_async_remote_copy(
            src_ref=carry.at[target],
            dst_ref=carry_land.at[k],
            send_sem=carry_send.at[k],
            recv_sem=carry_recv.at[k],
            device_id={"tm": target},
            device_id_type=MESH,
        )
        copy.start()
        carries.append(copy)

    total = half[0]
    for k, copy in enumerate(sends):
        copy.wait()
        total = total + land[k + 1]
    total = jnp.concatenate([total[j] for j in range(halves)], 1)
    inputs = matmul3(total, gain[...])

    entering = carry[me]
    for k, copy in enumerate(carries):
        copy.wait()
        entering = entering + carry_land[k + 1]

    first = put_row(jnp.zeros_like(inputs), entering[0:1], 0)
    filtered = inputs + matmul3(first, filt[0])
    for h in range(depth):
        filtered = filtered + matmul3(shift(filtered, 1 << h), filt[h])
    filtered_ref[...] = filtered
    following = put_row(jnp.zeros_like(inputs), entering[1:2], length - 1)
    smoothed = filtered + matmul3(following - filtered, back[0])
    for h in range(depth):
        smoothed = smoothed + matmul3(shift(smoothed, -(1 << h)), back[h])
    smoothed_ref[...] = smoothed


def per_device(
    gauge_series, gauge_order, gauge_block, gauge_weight, filt_trans, obs_gain, smooth_gain
):
    devices = lax.axis_size("tm")
    steps, columns = gauge_series.shape
    states = filt_trans.shape[0]
    length = steps // devices
    chips = devices // 2
    depth = length.bit_length() - 1
    scans = devices.bit_length() - 1
    halves = states // LANES
    out = jax.ShapeDtypeStruct((length, states), jnp.float32)
    square = (states, states)
    return pl.pallas_call(
        functools.partial(kernel, devices),
        out_shape=(out, out),
        in_specs=[pl.BlockSpec(memory_space=pltpu.VMEM)] * 7,
        out_specs=[pl.BlockSpec(memory_space=pltpu.VMEM)] * 2,
        scratch_shapes=[
            pltpu.VMEM((halves, steps, LANES), jnp.float32),
            pltpu.VMEM((chips, halves, length, LANES), jnp.float32),
            pltpu.VMEM((chips, halves, length, LANES), jnp.float32),
            pltpu.VMEM((devices, 2, states), jnp.float32),
            pltpu.VMEM((devices, 2, states), jnp.float32),
            pltpu.VMEM((depth + scans,) + square, jnp.float32),
            pltpu.VMEM((depth + scans,) + square, jnp.float32),
            pltpu.VMEM((depth,) + square, jnp.float32),
            pltpu.VMEM(square, jnp.float32),
            pltpu.VMEM(square, jnp.float32),
            pltpu.VMEM((steps, states), jnp.float32),
            pltpu.VMEM((steps, states), jnp.float32),
            pltpu.VMEM((2, devices, states), jnp.float32),
            pltpu.SemaphoreType.DMA((chips,)),
            pltpu.SemaphoreType.DMA((chips,)),
            pltpu.SemaphoreType.DMA((chips,)),
            pltpu.SemaphoreType.DMA((chips,)),
            pltpu.SemaphoreType.DMA((devices,)),
            pltpu.SemaphoreType.DMA((devices,)),
        ],
        compiler_params=pltpu.CompilerParams(
            collective_id=0, has_side_effects=True, vmem_limit_bytes=56 << 20
        ),
    )(
        gauge_series,
        gauge_order.reshape(devices, 1, columns),
        gauge_block.reshape(1, -1),
        gauge_weight.T,
        filt_trans,
        obs_gain,
        smooth_gain,
    )


def solution(mesh):
    placed = (
        P("groups", "tm"),
        P(),
        P(),
        P(),
        P("groups", None),
        P("groups", None),
        P("groups", None),
    )
    return jax.shard_map(
        per_device,
        mesh=mesh,
        in_specs=placed,
        out_specs=(P(("groups", "tm"), None), P(("groups", "tm"), None)),
        check_vma=False,
    )
```
